512 devices in a mesh: ctx: 32 (over z, y_hi), heads: 16 (over y_lo, x, core).
Axes of the slice: x: 4, y: 4 (y_hi: 2, y_lo: 2; y = y_hi * 2 + y_lo), z: 16, core: 2. Of those that a mesh axis runs over, the one named last changes fastest.
Arguments:
- queries: bfloat16 [8192, 4096], P('ctx', 'heads'), may hold values from -15 to 15
- prefix_keys: bfloat16 [7680, 2048], P('ctx', 'heads'), may hold values from -6 to 6
- prefix_values: bfloat16 [7680, 2048], P('ctx', 'heads'), may hold values from -6 to 6
- suffix_keys: bfloat16 [8192, 2048], P('ctx', 'heads'), may hold values from -10 to 10
- suffix_values: bfloat16 [8192, 2048], P('ctx', 'heads'), may hold values from -6 to 6
- out_weight: bfloat16 [4096, 4608], P('heads'), may hold values from -0.09375 to 0.09375
- lengths: int32 [16], replicated, may hold values from 128 to 512, as said below
- caps: float32 [16], replicated, may hold values from 8 to 50
Outputs:
- attended: float32 [8192, 4608], P(('ctx', 'heads'))
The draws below stay inside these ranges and needn't reach their ends.
Inputs may be any that keep to these rules, and one draw needn't show every extreme that they name: `lengths`: in every draw at least one request fills all 512 slots.
All inputs are finite; a program needn't handle non-finite values.
Results may differ from the reference program's by a relative error of at most 0.02.
Values may be sent and summed in bfloat16 or wider, within the bound.
No kernel may reach another device: no remote copies, remote signals or barrier semaphores. Data moves between devices by JAX's collectives and lax.ppermute only.
A program may use at most 64 MiB of HBM per device.

```python
import math
import jax
import jax.numpy as jnp
from jax import lax

D = 4608
HD = 128
GROUP = 2
KV_DEV = 1
SUF = 512
KVH = 16
QH = 32
PRE = 7680
TOKS = 8192
REQUESTS = 16
N_HEADS = 16


def draw_lengths(key, part):
    key = jax.random.fold_in(key, 7)
    spread_key, pick_key = jax.random.split(key)
    sampled = jax.random.randint(spread_key, (REQUESTS,), SUF // 4, SUF + 1)
    longest = jax.random.randint(pick_key, (), 0, REQUESTS)
    return jnp.where(jnp.arange(REQUESTS) == longest, SUF, sampled).astype(jnp.int32)


def block_levels(key, shape, cuts, smallest, top_value):
    def one(dim, parts):
        steps = jax.random.uniform(jax.random.fold_in(jax.random.fold_in(key, 6), dim), (parts,), jnp.float32, smallest / len(cuts), top_value / len(cuts))
        return jnp.repeat(jnp.exp(steps), shape[dim] // parts).reshape((-1,) + (1,) * (len(shape) - dim - 1))

    gain = one(*cuts[0])
    for cut in cuts[1:]:
        gain = gain * one(*cut)
    return gain


def bell_draw(key, extent, deviation, bound, cuts=(), kind=jnp.bfloat16):
    values = deviation * jax.random.normal(key, extent, jnp.float32)
    if cuts:
        values = values * block_levels(key, extent, cuts, -0.22, 0.18)
    return jnp.clip(values, -bound, bound).astype(kind)


def setup_inputs(seed: int = 0) -> dict:
    splits = jax.random.split(jax.random.key(seed), 9)
    queries = bell_draw(splits[0], (TOKS, QH * HD), 2.5, 15.0, ((0, 32), (1, 16)))
    prefix_keys = bell_draw(splits[1], (PRE, KVH * HD), 1.0, 6.0, ((0, 32), (1, 16)))
    prefix_values = bell_draw(splits[2], (PRE, KVH * HD), 1.0, 6.0, ((0, 32), (1, 16)))
    suffix_keys = bell_draw(splits[3], (TOKS, KVH * HD), 1.6, 10.0, ((0, 32), (1, 16)))
    suffix_values = bell_draw(splits[4], (TOKS, KVH * HD), 1.0, 6.0, ((0, 32), (1, 16)))
    out_weight = bell_draw(splits[5], (QH * HD, D), (QH * HD) ** -0.5, 0.09375, ((0, 16),))
    lengths = draw_lengths(jax.random.fold_in(splits[8], 71), 0)
    caps = jnp.clip(jnp.exp(jax.random.uniform(splits[7], (REQUESTS,), jnp.float32, math.log(8.0), math.log(50.0))), 8.0, 50.0)
    return dict(queries=queries, prefix_keys=prefix_keys, prefix_values=prefix_values, suffix_keys=suffix_keys, suffix_values=suffix_values, out_weight=out_weight, lengths=lengths, caps=caps)


score_scale = 1.0 / 12.0


def reference(queries, prefix_keys, prefix_values, suffix_keys, suffix_values, out_weight, lengths, caps):
    query_heads = queries.reshape(REQUESTS, SUF, KVH, GROUP, HD).transpose(2, 0, 1, 3, 4).reshape(KVH, REQUESTS, SUF * GROUP, HD)
    doc_keys = prefix_keys.reshape(PRE, KVH, HD).transpose(1, 0, 2)
    doc_values = prefix_values.reshape(PRE, KVH, HD).transpose(1, 0, 2)
    new_keys = suffix_keys.reshape(REQUESTS, SUF, KVH, HD).transpose(2, 0, 1, 3)
    new_values = suffix_values.reshape(REQUESTS, SUF, KVH, HD).transpose(2, 0, 1, 3)
    query_place = jnp.arange(SUF * GROUP, dtype=jnp.int32) // GROUP
    key_place = jnp.arange(SUF, dtype=jnp.int32)

    def one_head(head_items):
        head_queries, head_doc_keys, head_doc_values, head_new_keys, head_new_values = head_items

        def one_request(request_items):
            request_queries, request_keys, request_values, length, soft_cap = request_items
            raw_doc = jnp.dot(request_queries, head_doc_keys.T, preferred_element_type=jnp.float32)
            raw_new = jnp.dot(request_queries, request_keys.T, preferred_element_type=jnp.float32)
            weight_doc = jnp.exp(soft_cap * jnp.tanh(raw_doc * score_scale / soft_cap))
            visible = (key_place[None, :] <= query_place[:, None]) & (key_place[None, :] < length)
            weight_new = jnp.where(visible, jnp.exp(soft_cap * jnp.tanh(raw_new * score_scale / soft_cap)), 0.0)
            total = jnp.sum(weight_doc, axis=1) + jnp.sum(weight_new, axis=1)
            summed = jnp.dot(weight_doc.astype(jnp.bfloat16), head_doc_values, preferred_element_type=jnp.float32)
            summed = summed + jnp.dot(weight_new.astype(jnp.bfloat16), request_values, preferred_element_type=jnp.float32)
            return (summed / total[:, None]).astype(jnp.bfloat16)

        return lax.map(one_request, (head_queries, head_new_keys, head_new_values, lengths, caps))

    mixed = lax.map(one_head, (query_heads, doc_keys, doc_values, new_keys, new_values))
    mixed = mixed.reshape(KVH, REQUESTS, SUF, GROUP, HD).transpose(1, 2, 0, 3, 4).reshape(TOKS, QH * HD)
    group_cols = GROUP * KV_DEV * HD

    def add_group(accum, group_index):
        start = (group_index * group_cols).astype(jnp.int32)
        cols = lax.dynamic_slice_in_dim(mixed, start, group_cols, 1)
        rows = lax.dynamic_slice_in_dim(out_weight, start, group_cols, 0)
        partial_low = jnp.dot(cols, rows, preferred_element_type=jnp.float32).astype(jnp.bfloat16)
        partial_low = lax.optimization_barrier(partial_low)
        return accum + partial_low.astype(jnp.float32), None

    accum, unused = lax.scan(add_group, jnp.zeros((TOKS, D), jnp.float32), jnp.arange(N_HEADS, dtype=jnp.int32))
    return accum
```

```python
import functools
import math

import jax
import jax.numpy as jnp
from jax import lax
from jax.experimental import pallas as pl
from jax.experimental.pallas import tpu as pltpu
from jax.sharding import Mesh
from jax.sharding import PartitionSpec as P

HD = 128
GROUP = 2
SCALE = 1.0 / 12.0
LOG2E = math.log2(math.e)

AXES = ("z321", "z0", "yh", "yl", "x", "c")
SIZES = (8, 2, 2, 2, 4, 2)
CTX = ("z321", "z0", "yh")
HEADS = ("yl", "x", "c")
KEY_AXES = ("z321",)
QUERY_AXES = ("z0", "yh")
PEERS = 4
CHUNK = 640
PIECE = 16
META = 16


def attend_kernel(meta, caps, lengths, q_ref, kv_ref, own_ref, out_ref, acc_ref):
    peer = pl.program_id(0)
    head = pl.program_id(1)
    tokens = q_ref.shape[1]
    keys = kv_ref.shape[0]
    z_base, my_z0, my_yh = meta[0], meta[1], meta[2]
    peer_z0 = peer // 2
    peer_yh = lax.rem(peer, 2)
    request = z_base + peer_z0
    cap = jnp.full((1, 1), caps[request], jnp.float32)
    inner = SCALE / cap
    outer = cap * LOG2E
    q = q_ref[0]

    def weigh(k):
        raw = lax.dot_general(
            q, k, (((1,), (1,)), ((), ())), preferred_element_type=jnp.float32
        )
        return jnp.exp2(outer * jnp.tanh(raw * inner))

    def gather(w, v):
        ones = jnp.ones_like(v)
        return jnp.dot(
            w.astype(jnp.bfloat16),
            jnp.concatenate([v, ones], axis=1),
            preferred_element_type=jnp.float32,
        )

    total = None
    for start in range(0, keys, CHUNK):
        w = weigh(kv_ref[start : start + CHUNK, :HD])
        part = gather(w, kv_ref[start : start + CHUNK, HD:])
        total = part if total is None else total + part
    acc_ref[...] = total

    @pl.when((peer_z0 == my_z0) & (peer_yh >= my_yh))
    def _():
        new_keys = own_ref.shape[0]
        w = weigh(own_ref[:, :HD])
        row = peer_yh * tokens + lax.broadcasted_iota(jnp.int32, w.shape, 0)
        col = my_yh * new_keys + lax.broadcasted_iota(jnp.int32, w.shape, 1)
        seen = (col <= row) & (col < lengths[request])
        acc_ref[...] += gather(jnp.where(seen, w, 0.0), own_ref[:, HD:])

    for c in range(2):
        for j in range(tokens // (2 * PIECE)):
            rows = (2 * j + c) * PIECE
            out_ref[c, j * PIECE : (j + 1) * PIECE, :] = acc_ref[
                rows : rows + PIECE, :HD
            ].astype(out_ref.dtype)
        half = jnp.concatenate(
            [
                acc_ref[(2 * j + c) * PIECE : (2 * j + c + 1) * PIECE, HD:]
                for j in range(tokens // (2 * PIECE))
            ],
            axis=0,
        ).T[:META]
        high = half.astype(jnp.bfloat16).astype(jnp.float32)
        index = lax.broadcasted_iota(jnp.int32, half.shape, 0)
        out_ref[c, tokens // 2 :, :] = jnp.where(index == 0, high, half - high).astype(
            out_ref.dtype
        )


def attend(meta, caps, lengths, q, kv, own):
    peers, tokens, _ = q.shape
    keys = kv.shape[0]
    smem = pl.BlockSpec(memory_space=pltpu.SMEM)
    elements = peers * tokens * GROUP * (keys + own.shape[0] // 2)
    return pl.pallas_call(
        attend_kernel,
        out_shape=jax.ShapeDtypeStruct(
            (peers * 2, tokens // 2 + META, GROUP * HD), jnp.bfloat16
        ),
        grid=(peers, GROUP),
        in_specs=[
            smem,
            smem,
            smem,
            pl.BlockSpec((1, tokens, HD), lambda p, h: (p, 0, h)),
            pl.BlockSpec(kv.shape, lambda p, h: (0, 0)),
            pl.BlockSpec(own.shape, lambda p, h: (0, 0)),
        ],
        out_specs=pl.BlockSpec((2, tokens // 2 + META, HD), lambda p, h: (p, 0, h)),
        scratch_shapes=[pltpu.VMEM((tokens, 2 * HD), jnp.float32)],
        compiler_params=pltpu.CompilerParams(
            dimension_semantics=("arbitrary", "arbitrary"),
            vmem_limit_bytes=40 * 1024 * 1024,
        ),
        cost_estimate=pl.CostEstimate(
            flops=elements * HD * 4,
            bytes_accessed=4 * 1024 * 1024,
            transcendentals=elements * 2,
        ),
        name="attend",
    )(meta, caps, lengths, q, kv, own)


def project_kernel(meta, parts_ref, mine_ref, other_ref, out_ref, mixed_ref):
    half = parts_ref.shape[1] - META
    sources = parts_ref.shape[0] // 2

    @pl.when(pl.program_id(0) == 0)
    def _():
        for core in range(2):
            slot = jnp.where(meta[3] == core, 0, 1)
            for head in range(GROUP):
                cols = slice(head * HD, (head + 1) * HD)
                summed = jnp.zeros((half, HD), jnp.float32)
                totals = jnp.zeros((1, HD), jnp.float32)
                for s in range(sources):
                    block = parts_ref.at[2 * s + core]
                    summed += block[:half, cols].astype(jnp.float32)
                    pair = block[half:, cols].astype(jnp.float32)
                    totals += pair[0:1] + pair[1:2]
                column = jnp.broadcast_to(totals, (HD, HD)).T
                mixed_ref[slot, :, cols] = (summed / column).astype(jnp.bfloat16)

    total = jnp.dot(mixed_ref[0], mine_ref[...], preferred_element_type=jnp.float32)
    total += jnp.dot(mixed_ref[1], other_ref[...], preferred_element_type=jnp.float32)
    out_ref[...] = total.astype(out_ref.dtype)


def project(meta, parts, mine, other):
    half = parts.shape[1] - META
    depth, width = mine.shape
    block = 768
    return pl.pallas_call(
        project_kernel,
        out_shape=jax.ShapeDtypeStruct((half, width), jnp.bfloat16),
        grid=(width // block,),
        in_specs=[
            pl.BlockSpec(memory_space=pltpu.SMEM),
            pl.BlockSpec(parts.shape, lambda i: (0, 0, 0)),
            pl.BlockSpec((depth, block), lambda i: (0, i)),
            pl.BlockSpec((depth, block), lambda i: (0, i)),
        ],
        out_specs=pl.BlockSpec((half, block), lambda i: (0, i)),
        scratch_shapes=[pltpu.VMEM((2, half, GROUP * HD), jnp.bfloat16)],
        compiler_params=pltpu.CompilerParams(
            dimension_semantics=("arbitrary",), vmem_limit_bytes=40 * 1024 * 1024
        ),
        cost_estimate=pl.CostEstimate(
            flops=4 * half * depth * width,
            bytes_accessed=8 * 1024 * 1024,
            transcendentals=0,
        ),
        name="project",
    )(meta, parts, mine, other)


def local(
    queries, prefix_keys, prefix_values, suffix_keys, suffix_values, out_weight, lengths, caps
):
    tokens = queries.shape[0]
    meta = jnp.stack(
        [
            lax.axis_index("z321") * 2,
            lax.axis_index("z0"),
            lax.axis_index("yh"),
            lax.axis_index("c"),
        ]
    ).astype(jnp.int32)
    with jax.named_scope("queries_to_peers"):
        q = lax.all_to_all(
            jnp.broadcast_to(queries[None], (PEERS,) + queries.shape), QUERY_AXES, 0, 0, tiled=True
        )
    with jax.named_scope("weight_swap"):
        other_weight = lax.ppermute(out_weight, "c", [(0, 1), (1, 0)])
    with jax.named_scope("document_gather"):
        kv = lax.all_gather(
            jnp.concatenate([prefix_keys, prefix_values], axis=1), KEY_AXES, axis=0, tiled=True
        )
    own = jnp.concatenate([suffix_keys, suffix_values], axis=1)
    parts = attend(meta, caps, lengths, q, kv, own)
    with jax.named_scope("partials_to_owner"):
        parts = lax.all_to_all(parts, ("z0", "yh", "c"), 0, 0, tiled=True)
    partial = project(meta, parts, out_weight, other_weight)
    with jax.named_scope("heads_exchange"):
        pieces = lax.all_to_all(
            partial.reshape(8, PIECE, -1), ("yl", "x"), 0, 0, tiled=True
        )
    return jnp.sum(pieces.astype(jnp.float32), axis=0)


def solution(mesh):
    fine = Mesh(mesh.devices.reshape(SIZES), AXES)
    return jax.shard_map(
        local,
        mesh=fine,
        in_specs=(
            P(CTX, HEADS),
            P(CTX, HEADS),
            P(CTX, HEADS),
            P(CTX, HEADS),
            P(CTX, HEADS),
            P(HEADS, None),
            P(),
            P(),
        ),
        out_specs=P(CTX + HEADS, None),
        check_vma=False,
    )
```

```python
import math

import jax
import jax.numpy as jnp
from jax import lax
from jax.experimental import pallas as pl
from jax.experimental.pallas import tpu as pltpu
from jax.sharding import Mesh
from jax.sharding import PartitionSpec as P

HD = 128
GROUP = 2
SCALE = 1.0 / 12.0
LOG2E = math.log2(math.e)

AXES = ("z321", "z0", "yh", "yl", "x", "c")
SIZES = (8, 2, 2, 2, 4, 2)
CTX = ("z321", "z0", "yh")
HEADS = ("yl", "x", "c")
KEY_AXES = ("z321",)
QUERY_AXES = ("z0", "yh")
PEERS = 4
PIECE = 16
META = 16
BLOCK = 768


def attend_kernel(
    meta, caps, lengths, q_ref, kv_ref, new_k_ref, new_v_ref, out_ref, acc_ref
):
    peer = pl.program_id(0)
    tokens = q_ref.shape[1]
    new_keys = new_k_ref.shape[0]
    z_base, my_z0, my_yh = meta[0], meta[1], meta[2]
    peer_z0 = peer // 2
    peer_yh = lax.rem(peer, 2)
    request = z_base + peer_z0
    cap = jnp.full((1, 1), caps[request], jnp.float32)
    inner = SCALE / cap
    outer = cap * LOG2E
    slot = peer
    q = jnp.concatenate(
        [q_ref[slot, :, h * HD : (h + 1) * HD].astype(jnp.bfloat16) for h in range(GROUP)], axis=0
    )

    def weigh(k):
        raw = lax.dot_general(
            q, k, (((1,), (1,)), ((), ())), preferred_element_type=jnp.float32
        )
        return jnp.exp2(outer * jnp.tanh(raw * inner))

    def gather(w, v):
        return jnp.dot(
            w.astype(jnp.bfloat16),
            jnp.concatenate([v, jnp.ones_like(v)], axis=1),
            preferred_element_type=jnp.float32,
        )

    acc_ref[...] = gather(weigh(kv_ref[:, :HD]), kv_ref[:, HD:])

    @pl.when((peer_z0 == my_z0) & (peer_yh >= my_yh))
    def _():
        w = weigh(new_k_ref[...])
        place = lax.broadcasted_iota(jnp.int32, w.shape, 0) % tokens
        row = peer_yh * tokens + place
        col = my_yh * new_keys + lax.broadcasted_iota(jnp.int32, w.shape, 1)
        seen = (col <= row) & (col < lengths[request])
        acc_ref[...] += gather(jnp.where(seen, w, 0.0), new_v_ref[...])

    groups = tokens // (2 * PIECE)
    for head in range(GROUP):
        cols = slice(head * HD, (head + 1) * HD)
        for c in range(2):
            rows = [head * tokens + (2 * j + c) * PIECE for j in range(groups)]
            for j in range(groups):
                out_ref[c, j * PIECE : (j + 1) * PIECE, cols] = acc_ref[
                    rows[j] : rows[j] + PIECE, :HD
                ].astype(out_ref.dtype)
            totals = jnp.concatenate(
                [acc_ref[r : r + PIECE, HD:] for r in rows], axis=0
            ).T[:META]
            high = totals.astype(jnp.bfloat16).astype(jnp.float32)
            index = lax.broadcasted_iota(jnp.int32, totals.shape, 0)
            out_ref[c, tokens // 2 :, cols] = jnp.where(
                index == 0, high, totals - high
            ).astype(out_ref.dtype)


def attend(meta, caps, lengths, q, kv, new_k, new_v):
    _, tokens, _ = q.shape
    keys = kv.shape[0]
    smem = pl.BlockSpec(memory_space=pltpu.SMEM)
    elements = PEERS * tokens * GROUP * (keys + new_k.shape[0] // 2)
    return pl.pallas_call(
        attend_kernel,
        out_shape=jax.ShapeDtypeStruct(
            (PEERS * 2, tokens // 2 + META, GROUP * HD), jnp.bfloat16
        ),
        grid=(PEERS,),
        in_specs=[
            smem,
            smem,
            smem,
            pl.BlockSpec(q.shape, lambda p: (0, 0, 0)),
            pl.BlockSpec(kv.shape, lambda p: (0, 0)),
            pl.BlockSpec(new_k.shape, lambda p: (0, 0)),
            pl.BlockSpec(new_v.shape, lambda p: (0, 0)),
        ],
        out_specs=pl.BlockSpec((2, tokens // 2 + META, GROUP * HD), lambda p: (p, 0, 0)),
        scratch_shapes=[pltpu.VMEM((GROUP * tokens, 2 * HD), jnp.float32)],
        compiler_params=pltpu.CompilerParams(
            dimension_semantics=("arbitrary",),
            vmem_limit_bytes=40 * 1024 * 1024,
        ),
        cost_estimate=pl.CostEstimate(
            flops=elements * HD * 4,
            bytes_accessed=4 * 1024 * 1024,
            transcendentals=elements * 2,
        ),
        name="attend",
    )(meta, caps, lengths, q, kv, new_k, new_v)


def project_kernel(meta, parts_ref, mine_ref, other_ref, out_ref):
    half = parts_ref.shape[1] - META
    sources = parts_ref.shape[0] // 2
    own_core = meta[3]

    def mix(core):
        heads = []
        for head in range(GROUP):
            cols = slice(head * HD, (head + 1) * HD)
            summed = jnp.zeros((half, HD), jnp.float32)
            totals = jnp.zeros((1, HD), jnp.float32)
            for s in range(sources):
                summed += parts_ref[2 * s + core, :half, cols].astype(jnp.float32)
                pair = parts_ref[2 * s + core, half:, cols].astype(jnp.float32)
                totals += pair[0:1] + pair[1:2]
            column = jnp.broadcast_to(totals, (HD, HD)).T
            heads.append((summed / column).astype(jnp.bfloat16))
        return jnp.concatenate(heads, axis=1)

    mine = mix(own_core)
    other = mix(1 - own_core)
    width = out_ref.shape[1]
    for start in range(0, width, BLOCK):
        cols = slice(start, start + BLOCK)
        total = jnp.dot(mine, mine_ref[:, cols], preferred_element_type=jnp.float32)
        total += jnp.dot(other, other_ref[:, cols], preferred_element_type=jnp.float32)
        out_ref[:, cols] = total.astype(out_ref.dtype)


def project(meta, parts, mine, other):
    half = parts.shape[1] - META
    depth, width = mine.shape
    vmem = pl.BlockSpec(memory_space=pltpu.VMEM)
    return pl.pallas_call(
        project_kernel,
        out_shape=jax.ShapeDtypeStruct((half, width), jnp.bfloat16),
        in_specs=[pl.BlockSpec(memory_space=pltpu.SMEM), vmem, vmem, vmem],
        out_specs=vmem,
        compiler_params=pltpu.CompilerParams(vmem_limit_bytes=40 * 1024 * 1024),
        cost_estimate=pl.CostEstimate(
            flops=4 * half * depth * width,
            bytes_accessed=8 * 1024 * 1024,
            transcendentals=0,
        ),
        name="project",
    )(meta, parts, mine, other)


def local(
    queries, prefix_keys, prefix_values, suffix_keys, suffix_values, out_weight, lengths, caps
):
    tokens = queries.shape[0]
    meta = jnp.stack(
        [
            lax.axis_index("z321") * 2,
            lax.axis_index("z0"),
            lax.axis_index("yh"),
            lax.axis_index("c"),
        ]
    ).astype(jnp.int32)
    q = lax.all_to_all(jnp.broadcast_to(queries[None], (PEERS,) + queries.shape), QUERY_AXES, 0, 0, tiled=True)
    weights = (out_weight, lax.ppermute(out_weight, "c", [(0, 1), (1, 0)]))
    with jax.named_scope("document_gather"):
        kv = lax.all_gather(
            jnp.concatenate([prefix_keys, prefix_values], axis=1), KEY_AXES, axis=0, tiled=True
        )
    parts = attend(meta, caps, lengths, q, kv, suffix_keys, suffix_values)
    with jax.named_scope("partials_to_owner"):
        parts = lax.all_to_all(parts, ("z0", "yh", "c"), 0, 0, tiled=True)
    partial = project(meta, parts, *weights)
    with jax.named_scope("heads_exchange"):
        pieces = lax.all_to_all(
            partial.reshape(8, PIECE, -1), ("yl", "x"), 0, 0, tiled=True
        )
    return jnp.sum(pieces.astype(jnp.float32), axis=0)


def solution(mesh):
    fine = Mesh(mesh.devices.reshape(SIZES), AXES)
    return jax.shard_map(
        local,
        mesh=fine,
        in_specs=(
            P(CTX, HEADS),
            P(CTX, HEADS),
            P(CTX, HEADS),
            P(CTX, HEADS),
            P(CTX, HEADS),
            P(HEADS, None),
            P(),
            P(),
        ),
        out_specs=P(CTX + HEADS, None),
        check_vma=False,
    )
```

```python
import math

import jax
import jax.numpy as jnp
from jax import lax
from jax.experimental import pallas as pl
from jax.experimental.pallas import tpu as pltpu
from jax.sharding import Mesh
from jax.sharding import PartitionSpec as P

HD = 128
GROUP = 2
SCALE = 1.0 / 12.0
LOG2E = math.log2(math.e)

AXES = ("z321", "z0", "yh", "yl", "x", "c")
SIZES = (8, 2, 2, 2, 4, 2)
CTX = ("z321", "z0", "yh")
HEADS = ("yl", "x", "c")
KEY_AXES = ("z321",)
QUERY_AXES = ("z0", "yh")
PEERS = 4
PIECE = 16
META = 16
BLOCK = 768


def prepare_kernel(q_ref, k_ref, v_ref, copies_ref, kv_ref):
    kv_ref[:, :HD] = k_ref[...]
    kv_ref[:, HD:] = v_ref[...]
    for peer in range(PEERS):
        copies_ref[peer] = q_ref[...]


def prepare(q, k, v):
    vmem = pl.BlockSpec(memory_space=pltpu.VMEM)
    return pl.pallas_call(
        prepare_kernel,
        out_shape=(
            jax.ShapeDtypeStruct((PEERS,) + q.shape, q.dtype),
            jax.ShapeDtypeStruct((k.shape[0], 2 * HD), k.dtype),
        ),
        in_specs=[vmem] * 3,
        out_specs=(vmem, vmem),
        name="prepare",
    )(q, k, v)


def attend_kernel(
    meta, caps, lengths, q_ref, kv_ref, new_k_ref, new_v_ref, out_ref, acc_ref
):
    def serve(peer):
        tokens = q_ref.shape[1]
        new_keys = new_k_ref.shape[0]
        z_base, my_z0, my_yh = meta[0], meta[1], meta[2]
        peer_z0 = peer // 2
        peer_yh = lax.rem(peer, 2)
        request = z_base + peer_z0
        cap = jnp.full((1, 1), caps[request], jnp.float32)
        inner = SCALE / cap
        outer = cap * LOG2E
        slot = peer
        q = jnp.concatenate(
            [q_ref[slot, :, h * HD : (h + 1) * HD].astype(jnp.bfloat16) for h in range(GROUP)], axis=0
        )

        def weigh(k):
            raw = lax.dot_general(
                q, k, (((1,), (1,)), ((), ())), preferred_element_type=jnp.float32
            )
            return jnp.exp2(outer * jnp.tanh(raw * inner))

        def gather(w, v):
            return jnp.dot(
                w.astype(jnp.bfloat16),
                jnp.concatenate([v, jnp.ones_like(v)], axis=1),
                preferred_element_type=jnp.float32,
            )

        def document():
            return gather(weigh(kv_ref[:, :HD]), kv_ref[:, HD:])

        def suffix():
            w = weigh(new_k_ref[...])
            place = lax.broadcasted_iota(jnp.int32, w.shape, 0) % tokens
            row = peer_yh * tokens + place
            col = my_yh * new_keys + lax.broadcasted_iota(jnp.int32, w.shape, 1)
            seen = (col <= row) & (col < lengths[request])
            return gather(jnp.where(seen, w, 0.0), new_v_ref[...])

        sees_suffix = (peer_z0 == my_z0) & (peer_yh >= my_yh)

        @pl.when(sees_suffix)
        def _():
            acc_ref[...] = suffix() + document()

        @pl.when(jnp.logical_not(sees_suffix))
        def _():
            acc_ref[...] = document()

        groups = tokens // (2 * PIECE)
        for head in range(GROUP):
            cols = slice(head * HD, (head + 1) * HD)
            for c in range(2):
                rows = [head * tokens + (2 * j + c) * PIECE for j in range(groups)]
                for j in range(groups):
                    out_ref[2 * peer + c, j * PIECE : (j + 1) * PIECE, cols] = acc_ref[
                        rows[j] : rows[j] + PIECE, :HD
                    ].astype(out_ref.dtype)
                totals = jnp.concatenate(
                    [acc_ref[r : r + PIECE, HD:] for r in rows], axis=0
                ).T[:META]
                high = totals.astype(jnp.bfloat16).astype(jnp.float32)
                index = lax.broadcasted_iota(jnp.int32, totals.shape, 0)
                out_ref[2 * peer + c, tokens // 2 :, cols] = jnp.where(
                    index == 0, high, totals - high
                ).astype(out_ref.dtype)

    def step(peer, carry):
        serve(peer)
        return carry

    lax.fori_loop(0, PEERS, step, 0)


def attend(meta, caps, lengths, q, kv, new_k, new_v):
    _, tokens, _ = q.shape
    keys = kv.shape[0]
    smem = pl.BlockSpec(memory_space=pltpu.SMEM)
    vmem = pl.BlockSpec(memory_space=pltpu.VMEM)
    elements = PEERS * tokens * GROUP * (keys + new_k.shape[0] // 2)
    return pl.pallas_call(
        attend_kernel,
        out_shape=jax.ShapeDtypeStruct(
            (PEERS * 2, tokens // 2 + META, GROUP * HD), jnp.bfloat16
        ),
        in_specs=[smem, smem, smem, vmem, vmem, vmem, vmem],
        out_specs=vmem,
        scratch_shapes=[pltpu.VMEM((GROUP * tokens, 2 * HD), jnp.float32)],
        compiler_params=pltpu.CompilerParams(
            vmem_limit_bytes=40 * 1024 * 1024,
        ),
        cost_estimate=pl.CostEstimate(
            flops=elements * HD * 4,
            bytes_accessed=4 * 1024 * 1024,
            transcendentals=elements * 2,
        ),
        name="attend",
    )(meta, caps, lengths, q, kv, new_k, new_v)


def project_kernel(meta, parts_ref, mine_ref, other_ref, out_ref):
    half = parts_ref.shape[1] - META
    sources = parts_ref.shape[0] // 2
    own_core = meta[3]

    def mix(core):
        heads = []
        for head in range(GROUP):
            cols = slice(head * HD, (head + 1) * HD)
            summed = jnp.zeros((half, HD), jnp.float32)
            totals = jnp.zeros((1, HD), jnp.float32)
            for s in range(sources):
                summed += parts_ref[2 * s + core, :half, cols].astype(jnp.float32)
                pair = parts_ref[2 * s + core, half:, cols].astype(jnp.float32)
                totals += pair[0:1] + pair[1:2]
            column = jnp.broadcast_to(totals, (HD, HD)).T
            heads.append((summed / column).astype(jnp.bfloat16))
        return jnp.concatenate(heads, axis=1)

    mine = mix(own_core)
    other = mix(1 - own_core)
    width = out_ref.shape[1]
    for start in range(0, width, BLOCK):
        cols = slice(start, start + BLOCK)
        total = jnp.dot(mine, mine_ref[:, cols], preferred_element_type=jnp.float32)
        total += jnp.dot(other, other_ref[:, cols], preferred_element_type=jnp.float32)
        out_ref[:, cols] = total.astype(out_ref.dtype)


def project(meta, parts, mine, other):
    half = parts.shape[1] - META
    depth, width = mine.shape
    vmem = pl.BlockSpec(memory_space=pltpu.VMEM)
    return pl.pallas_call(
        project_kernel,
        out_shape=jax.ShapeDtypeStruct((half, width), jnp.bfloat16),
        in_specs=[pl.BlockSpec(memory_space=pltpu.SMEM), vmem, vmem, vmem],
        out_specs=vmem,
        compiler_params=pltpu.CompilerParams(vmem_limit_bytes=40 * 1024 * 1024),
        cost_estimate=pl.CostEstimate(
            flops=4 * half * depth * width,
            bytes_accessed=8 * 1024 * 1024,
            transcendentals=0,
        ),
        name="project",
    )(meta, parts, mine, other)


def local(
    queries, prefix_keys, prefix_values, suffix_keys, suffix_values, out_weight, lengths, caps
):
    tokens = queries.shape[0]
    meta = jnp.stack(
        [
            lax.axis_index("z321") * 2,
            lax.axis_index("z0"),
            lax.axis_index("yh"),
            lax.axis_index("c"),
        ]
    ).astype(jnp.int32)
    copies, pair = prepare(queries, prefix_keys, prefix_values)
    q = lax.all_to_all(copies, QUERY_AXES, 0, 0, tiled=True)
    with jax.named_scope("document_gather"):
        kv = lax.all_gather(
            pair, KEY_AXES, axis=0, tiled=True
        )
    parts = attend(meta, caps, lengths, q, kv, suffix_keys, suffix_values)
    late_weight, parts = lax.optimization_barrier((out_weight, parts))
    with jax.named_scope("partials_to_owner"):
        parts = lax.all_to_all(parts, ("z0", "yh", "c"), 0, 0, tiled=True)
    weights = (out_weight, lax.ppermute(late_weight, "c", [(0, 1), (1, 0)]))
    partial = project(meta, parts, *weights)
    with jax.named_scope("heads_exchange"):
        pieces = lax.all_to_all(
            partial.reshape(8, PIECE, -1), ("yl", "x"), 0, 0, tiled=True
        )
    return jnp.sum(pieces.astype(jnp.float32), axis=0)


def solution(mesh):
    fine = Mesh(mesh.devices.reshape(SIZES), AXES)
    return jax.shard_map(
        local,
        mesh=fine,
        in_specs=(
            P(CTX, HEADS),
            P(CTX, HEADS),
            P(CTX, HEADS),
            P(CTX, HEADS),
            P(CTX, HEADS),
            P(HEADS, None),
            P(),
            P(),
        ),
        out_specs=P(CTX + HEADS, None),
        check_vma=False,
    )
```

```python
import math

import jax
import jax.numpy as jnp
from jax import lax
from jax.experimental import pallas as pl
from jax.experimental.pallas import tpu as pltpu
from jax.sharding import Mesh
from jax.sharding import PartitionSpec as P

HD = 128
GROUP = 2
SCALE = 1.0 / 12.0
LOG2E = math.log2(math.e)

AXES = ("z321", "z0", "yh", "yl", "x", "c")
SIZES = (8, 2, 2, 2, 4, 2)
CTX = ("z321", "z0", "yh")
HEADS = ("yl", "x", "c")
KEY_AXES = ("z321",)
QUERY_AXES = ("z0", "yh")
PEERS = 4
PIECE = 16
META = 16
BLOCK = 768


def prepare_kernel(q_ref, k_ref, v_ref, copies_ref, kv_ref):
    kv_ref[:, :HD] = k_ref[...]
    kv_ref[:, HD:] = v_ref[...]
    for peer in range(PEERS):
        copies_ref[peer] = q_ref[...]


def prepare(q, k, v):
    vmem = pl.BlockSpec(memory_space=pltpu.VMEM)
    return pl.pallas_call(
        prepare_kernel,
        out_shape=(
            jax.ShapeDtypeStruct((PEERS,) + q.shape, q.dtype),
            jax.ShapeDtypeStruct((k.shape[0], 2 * HD), k.dtype),
        ),
        in_specs=[vmem] * 3,
        out_specs=(vmem, vmem),
        name="prepare",
    )(q, k, v)


def attend_kernel(
    meta, caps, lengths, q_ref, kv_ref, new_k_ref, new_v_ref, out_ref, acc_ref, totals_ref
):
    totals_ref[...] = jnp.zeros_like(totals_ref)

    def serve(peer):
        tokens = q_ref.shape[1]
        new_keys = new_k_ref.shape[0]
        z_base, my_z0, my_yh = meta[0], meta[1], meta[2]
        peer_z0 = peer // 2
        peer_yh = lax.rem(peer, 2)
        request = z_base + peer_z0
        cap = jnp.full((1, 1), caps[request], jnp.float32)
        inner = SCALE / cap
        outer = cap * LOG2E
        slot = peer
        q = jnp.concatenate(
            [q_ref[slot, :, h * HD : (h + 1) * HD].astype(jnp.bfloat16) for h in range(GROUP)], axis=0
        )

        def weigh(k):
            raw = lax.dot_general(
                q, k, (((1,), (1,)), ((), ())), preferred_element_type=jnp.float32
            )
            return jnp.exp2(outer * jnp.tanh(raw * inner))

        def gather(w, v):
            return jnp.dot(
                w.astype(jnp.bfloat16),
                jnp.concatenate([v, jnp.ones_like(v)], axis=1),
                preferred_element_type=jnp.float32,
            )

        def document():
            return gather(weigh(kv_ref[:, :HD]), kv_ref[:, HD:])

        def suffix():
            w = weigh(new_k_ref[...])
            place = lax.broadcasted_iota(jnp.int32, w.shape, 0) % tokens
            row = peer_yh * tokens + place
            col = my_yh * new_keys + lax.broadcasted_iota(jnp.int32, w.shape, 1)
            seen = (col <= row) & (col < lengths[request])
            return gather(jnp.where(seen, w, 0.0), new_v_ref[...])

        sees_suffix = (peer_z0 == my_z0) & (peer_yh >= my_yh)

        @pl.when(sees_suffix)
        def _():
            acc_ref[...] = suffix() + document()

        @pl.when(jnp.logical_not(sees_suffix))
        def _():
            acc_ref[...] = document()

        groups = tokens // (2 * PIECE)
        for head in range(GROUP):
            cols = slice(head * HD, (head + 1) * HD)
            for c in range(2):
                rows = [head * tokens + (2 * j + c) * PIECE for j in range(groups)]
                for j in range(groups):
                    out_ref[2 * peer + c, j * PIECE : (j + 1) * PIECE, cols] = acc_ref[
                        rows[j] : rows[j] + PIECE, :HD
                    ].astype(out_ref.dtype)
                totals = jnp.concatenate([acc_ref[r : r + PIECE, HD:] for r in rows], axis=0)
                lane = lax.broadcasted_iota(jnp.int32, totals.shape, 1)
                place = (2 * peer + c) * GROUP + head
                totals_ref[...] = jnp.where(lane == place, totals, totals_ref[...])

    def step(peer, carry):
        serve(peer)
        return carry

    lax.fori_loop(0, PEERS, step, 0)

    low_rows = totals_ref[...].T[: 2 * PEERS * GROUP]
    high_rows = low_rows.astype(jnp.bfloat16).astype(jnp.float32)
    low_rows = low_rows - high_rows
    first = lax.broadcasted_iota(jnp.int32, (META, HD), 0) == 0
    for target in range(2 * PEERS):
        for head in range(GROUP):
            row = slice(target * GROUP + head, target * GROUP + head + 1)
            pair = jnp.where(first, high_rows[row], low_rows[row])
            out_ref[target, out_ref.shape[1] - META :, head * HD : (head + 1) * HD] = pair.astype(
                out_ref.dtype
            )


def attend(meta, caps, lengths, q, kv, new_k, new_v):
    _, tokens, _ = q.shape
    keys = kv.shape[0]
    smem = pl.BlockSpec(memory_space=pltpu.SMEM)
    vmem = pl.BlockSpec(memory_space=pltpu.VMEM)
    elements = PEERS * tokens * GROUP * (keys + new_k.shape[0] // 2)
    return pl.pallas_call(
        attend_kernel,
        out_shape=jax.ShapeDtypeStruct(
            (PEERS * 2, tokens // 2 + META, GROUP * HD), jnp.bfloat16
        ),
        in_specs=[smem, smem, smem, vmem, vmem, vmem, vmem],
        out_specs=vmem,
        scratch_shapes=[
            pltpu.VMEM((GROUP * tokens, 2 * HD), jnp.float32),
            pltpu.VMEM((tokens // 2, HD), jnp.float32),
        ],
        compiler_params=pltpu.CompilerParams(
            vmem_limit_bytes=40 * 1024 * 1024,
        ),
        cost_estimate=pl.CostEstimate(
            flops=elements * HD * 4,
            bytes_accessed=4 * 1024 * 1024,
            transcendentals=elements * 2,
        ),
        name="attend",
    )(meta, caps, lengths, q, kv, new_k, new_v)


def project_kernel(meta, parts_ref, mine_ref, other_ref, out_ref):
    half = parts_ref.shape[1] - META
    sources = parts_ref.shape[0] // 2
    own_core = meta[3]

    def mix(core):
        heads = []
        for head in range(GROUP):
            cols = slice(head * HD, (head + 1) * HD)
            summed = jnp.zeros((half, HD), jnp.float32)
            totals = jnp.zeros((1, HD), jnp.float32)
            for s in range(sources):
                summed += parts_ref[2 * s + core, :half, cols].astype(jnp.float32)
                pair = parts_ref[2 * s + core, half:, cols].astype(jnp.float32)
                totals += pair[0:1] + pair[1:2]
            column = jnp.broadcast_to(totals, (HD, HD)).T
            heads.append((summed / column).astype(jnp.bfloat16))
        return jnp.concatenate(heads, axis=1)

    mine = mix(own_core)
    other = mix(1 - own_core)
    width = out_ref.shape[1]
    for start in range(0, width, BLOCK):
        cols = slice(start, start + BLOCK)
        total = jnp.dot(mine, mine_ref[:, cols], preferred_element_type=jnp.float32)
        total += jnp.dot(other, other_ref[:, cols], preferred_element_type=jnp.float32)
        out_ref[:, cols] = total.astype(out_ref.dtype)


def project(meta, parts, mine, other):
    half = parts.shape[1] - META
    depth, width = mine.shape
    vmem = pl.BlockSpec(memory_space=pltpu.VMEM)
    return pl.pallas_call(
        project_kernel,
        out_shape=jax.ShapeDtypeStruct((half, width), jnp.bfloat16),
        in_specs=[pl.BlockSpec(memory_space=pltpu.SMEM), vmem, vmem, vmem],
        out_specs=vmem,
        compiler_params=pltpu.CompilerParams(vmem_limit_bytes=40 * 1024 * 1024),
        cost_estimate=pl.CostEstimate(
            flops=4 * half * depth * width,
            bytes_accessed=8 * 1024 * 1024,
            transcendentals=0,
        ),
        name="project",
    )(meta, parts, mine, other)


def local(
    queries, prefix_keys, prefix_values, suffix_keys, suffix_values, out_weight, lengths, caps
):
    tokens = queries.shape[0]
    meta = jnp.stack(
        [
            lax.axis_index("z321") * 2,
            lax.axis_index("z0"),
            lax.axis_index("yh"),
            lax.axis_index("c"),
        ]
    ).astype(jnp.int32)
    copies, pair = prepare(queries, prefix_keys, prefix_values)
    q = lax.all_to_all(copies, QUERY_AXES, 0, 0, tiled=True)
    with jax.named_scope("document_gather"):
        kv = lax.all_gather(
            pair, KEY_AXES, axis=0, tiled=True
        )
    parts = attend(meta, caps, lengths, q, kv, suffix_keys, suffix_values)
    late_weight, parts = lax.optimization_barrier((out_weight, parts))
    with jax.named_scope("partials_to_owner"):
        parts = lax.all_to_all(parts, ("z0", "yh", "c"), 0, 0, tiled=True)
    weights = (out_weight, lax.ppermute(late_weight, "c", [(0, 1), (1, 0)]))
    partial = project(meta, parts, *weights)
    with jax.named_scope("heads_exchange"):
        pieces = lax.all_to_all(
            partial.reshape(8, PIECE, -1), ("yl", "x"), 0, 0, tiled=True
        )
    return jnp.sum(pieces.astype(jnp.float32), axis=0)


def solution(mesh):
    fine = Mesh(mesh.devices.reshape(SIZES), AXES)
    return jax.shard_map(
        local,
        mesh=fine,
        in_specs=(
            P(CTX, HEADS),
            P(CTX, HEADS),
            P(CTX, HEADS),
            P(CTX, HEADS),
            P(CTX, HEADS),
            P(HEADS, None),
            P(),
            P(),
        ),
        out_specs=P(CTX + HEADS, None),
        check_vma=False,
    )
```

```python
import math

import jax
import jax.numpy as jnp
from jax import lax
from jax.experimental import pallas as pl
from jax.experimental.pallas import tpu as pltpu
from jax.sharding import Mesh
from jax.sharding import PartitionSpec as P

HD = 128
GROUP = 2
SCALE = 1.0 / 12.0
LOG2E = math.log2(math.e)

AXES = ("z321", "z0", "yh", "yl", "x", "c")
SIZES = (8, 2, 2, 2, 4, 2)
CTX = ("z321", "z0", "yh")
HEADS = ("yl", "x", "c")
KEY_AXES = ("z321",)
QUERY_AXES = ("z0", "yh")
PEERS = 4
PIECE = 16
META = 16
BLOCK = 768


def prepare_kernel(q_ref, k_ref, v_ref, copies_ref, kv_ref):
    kv_ref[:, :HD] = k_ref[...]
    kv_ref[:, HD:] = v_ref[...]
    for peer in range(PEERS):
        copies_ref[peer] = q_ref[...]


def prepare(q, k, v):
    vmem = pl.BlockSpec(memory_space=pltpu.VMEM)
    return pl.pallas_call(
        prepare_kernel,
        out_shape=(
            jax.ShapeDtypeStruct((PEERS,) + q.shape, q.dtype),
            jax.ShapeDtypeStruct((k.shape[0], 2 * HD), k.dtype),
        ),
        in_specs=[vmem] * 3,
        out_specs=(vmem, vmem),
        name="prepare",
    )(q, k, v)


def attend_kernel(
    meta, caps, lengths, q_ref, kv_ref, new_k_ref, new_v_ref, out_ref, acc_ref, totals_ref
):
    totals_ref[...] = jnp.zeros_like(totals_ref)

    def serve(peer):
        tokens = q_ref.shape[1]
        new_keys = new_k_ref.shape[0]
        z_base, my_z0, my_yh = meta[0], meta[1], meta[2]
        peer_z0 = peer // 2
        peer_yh = peer % 2
        request = z_base + peer_z0
        cap = jnp.full((1, 1), caps[request], jnp.float32)
        inner = SCALE / cap
        outer = cap * LOG2E
        slot = peer
        q = jnp.concatenate(
            [q_ref[slot, :, h * HD : (h + 1) * HD].astype(jnp.bfloat16) for h in range(GROUP)], axis=0
        )

        def weigh(k):
            raw = lax.dot_general(
                q, k, (((1,), (1,)), ((), ())), preferred_element_type=jnp.float32
            )
            return jnp.exp2(outer * jnp.tanh(raw * inner))

        def gather(w, v):
            return jnp.dot(
                w.astype(jnp.bfloat16),
                jnp.concatenate([v, jnp.ones_like(v)], axis=1),
                preferred_element_type=jnp.float32,
            )

        def document():
            return gather(weigh(kv_ref[:, :HD]), kv_ref[:, HD:])

        def suffix():
            w = weigh(new_k_ref[...])
            place = lax.broadcasted_iota(jnp.int32, w.shape, 0) % tokens
            row = peer_yh * tokens + place
            col = my_yh * new_keys + lax.broadcasted_iota(jnp.int32, w.shape, 1)
            seen = (col <= row) & (col < lengths[request])
            return gather(jnp.where(seen, w, 0.0), new_v_ref[...])

        sees_suffix = (peer_z0 == my_z0) & (peer_yh >= my_yh)

        @pl.when(sees_suffix)
        def _():
            acc_ref[...] = suffix() + document()

        @pl.when(jnp.logical_not(sees_suffix))
        def _():
            acc_ref[...] = document()

        groups = tokens // (2 * PIECE)
        for head in range(GROUP):
            cols = slice(head * HD, (head + 1) * HD)
            for c in range(2):
                rows = [head * tokens + (2 * j + c) * PIECE for j in range(groups)]
                for j in range(groups):
                    out_ref[2 * peer + c, j * PIECE : (j + 1) * PIECE, cols] = acc_ref[
                        rows[j] : rows[j] + PIECE, :HD
                    ].astype(out_ref.dtype)
                totals = jnp.concatenate([acc_ref[r : r + PIECE, HD:] for r in rows], axis=0)
                lane = lax.broadcasted_iota(jnp.int32, totals.shape, 1)
                place = (2 * peer + c) * GROUP + head
                totals_ref[...] = jnp.where(lane == place, totals, totals_ref[...])

    for peer in range(PEERS):
        serve(peer)

    low_rows = totals_ref[...].T[: 2 * PEERS * GROUP]
    high_rows = low_rows.astype(jnp.bfloat16).astype(jnp.float32)
    low_rows = low_rows - high_rows
    first = lax.broadcasted_iota(jnp.int32, (META, HD), 0) == 0
    for target in range(2 * PEERS):
        for head in range(GROUP):
            row = slice(target * GROUP + head, target * GROUP + head + 1)
            pair = jnp.where(first, high_rows[row], low_rows[row])
            out_ref[target, out_ref.shape[1] - META :, head * HD : (head + 1) * HD] = pair.astype(
                out_ref.dtype
            )


def attend(meta, caps, lengths, q, kv, new_k, new_v):
    _, tokens, _ = q.shape
    keys = kv.shape[0]
    smem = pl.BlockSpec(memory_space=pltpu.SMEM)
    vmem = pl.BlockSpec(memory_space=pltpu.VMEM)
    elements = PEERS * tokens * GROUP * (keys + new_k.shape[0] // 2)
    return pl.pallas_call(
        attend_kernel,
        out_shape=jax.ShapeDtypeStruct(
            (PEERS * 2, tokens // 2 + META, GROUP * HD), jnp.bfloat16
        ),
        in_specs=[smem, smem, smem, vmem, vmem, vmem, vmem],
        out_specs=vmem,
        scratch_shapes=[
            pltpu.VMEM((GROUP * tokens, 2 * HD), jnp.float32),
            pltpu.VMEM((tokens // 2, HD), jnp.float32),
        ],
        compiler_params=pltpu.CompilerParams(
            vmem_limit_bytes=40 * 1024 * 1024,
        ),
        cost_estimate=pl.CostEstimate(
            flops=elements * HD * 4,
            bytes_accessed=4 * 1024 * 1024,
            transcendentals=elements * 2,
        ),
        name="attend",
    )(meta, caps, lengths, q, kv, new_k, new_v)


def project_kernel(meta, parts_ref, mine_ref, other_ref, out_ref):
    half = parts_ref.shape[1] - META
    sources = parts_ref.shape[0] // 2
    own_core = meta[3]

    def mix(core):
        heads = []
        for head in range(GROUP):
            cols = slice(head * HD, (head + 1) * HD)
            summed = jnp.zeros((half, HD), jnp.float32)
            totals = jnp.zeros((1, HD), jnp.float32)
            for s in range(sources):
                summed += parts_ref[2 * s + core, :half, cols].astype(jnp.float32)
                pair = parts_ref[2 * s + core, half:, cols].astype(jnp.float32)
                totals += pair[0:1] + pair[1:2]
            column = jnp.broadcast_to(totals, (HD, HD)).T
            heads.append((summed / column).astype(jnp.bfloat16))
        return jnp.concatenate(heads, axis=1)

    mine = mix(own_core)
    other = mix(1 - own_core)
    width = out_ref.shape[1]
    for start in range(0, width, BLOCK):
        cols = slice(start, start + BLOCK)
        total = jnp.dot(mine, mine_ref[:, cols], preferred_element_type=jnp.float32)
        total += jnp.dot(other, other_ref[:, cols], preferred_element_type=jnp.float32)
        out_ref[:, cols] = total.astype(out_ref.dtype)


def project(meta, parts, mine, other):
    half = parts.shape[1] - META
    depth, width = mine.shape
    vmem = pl.BlockSpec(memory_space=pltpu.VMEM)
    return pl.pallas_call(
        project_kernel,
        out_shape=jax.ShapeDtypeStruct((half, width), jnp.bfloat16),
        in_specs=[pl.BlockSpec(memory_space=pltpu.SMEM), vmem, vmem, vmem],
        out_specs=vmem,
        compiler_params=pltpu.CompilerParams(vmem_limit_bytes=40 * 1024 * 1024),
        cost_estimate=pl.CostEstimate(
            flops=4 * half * depth * width,
            bytes_accessed=8 * 1024 * 1024,
            transcendentals=0,
        ),
        name="project",
    )(meta, parts, mine, other)


def local(
    queries, prefix_keys, prefix_values, suffix_keys, suffix_values, out_weight, lengths, caps
):
    tokens = queries.shape[0]
    meta = jnp.stack(
        [
            lax.axis_index("z321") * 2,
            lax.axis_index("z0"),
            lax.axis_index("yh"),
            lax.axis_index("c"),
        ]
    ).astype(jnp.int32)
    copies, pair = prepare(queries, prefix_keys, prefix_values)
    q = lax.all_to_all(copies, QUERY_AXES, 0, 0, tiled=True)
    with jax.named_scope("document_gather"):
        kv = lax.all_gather(
            pair, KEY_AXES, axis=0, tiled=True
        )
    parts = attend(meta, caps, lengths, q, kv, suffix_keys, suffix_values)
    late_weight, parts = lax.optimization_barrier((out_weight, parts))
    with jax.named_scope("partials_to_owner"):
        parts = lax.all_to_all(parts, ("z0", "yh", "c"), 0, 0, tiled=True)
    weights = (out_weight, lax.ppermute(late_weight, "c", [(0, 1), (1, 0)]))
    partial = project(meta, parts, *weights)
    with jax.named_scope("heads_exchange"):
        pieces = lax.all_to_all(
            partial.reshape(8, PIECE, -1), ("yl", "x"), 0, 0, tiled=True
        )
    return jnp.sum(pieces.astype(jnp.float32), axis=0)


def solution(mesh):
    fine = Mesh(mesh.devices.reshape(SIZES), AXES)
    return jax.shard_map(
        local,
        mesh=fine,
        in_specs=(
            P(CTX, HEADS),
            P(CTX, HEADS),
            P(CTX, HEADS),
            P(CTX, HEADS),
            P(CTX, HEADS),
            P(HEADS, None),
            P(),
            P(),
        ),
        out_specs=P(CTX + HEADS, None),
        check_vma=False,
    )
```

```python
import math

import jax
import jax.numpy as jnp
from jax import lax
from jax.experimental import pallas as pl
from jax.experimental.pallas import tpu as pltpu
from jax.sharding import Mesh
from jax.sharding import PartitionSpec as P

HD = 128
GROUP = 2
SCALE = 1.0 / 12.0
LOG2E = math.log2(math.e)

AXES = ("z321", "z0", "yh", "yl", "x", "c")
SIZES = (8, 2, 2, 2, 4, 2)
CTX = ("z321", "z0", "yh")
HEADS = ("yl", "x", "c")
KEY_AXES = ("z321",)
QUERY_AXES = ("z0", "yh")
PEERS = 4
PIECE = 16
META = 16
BLOCK = 1536


def prepare_kernel(q_ref, k_ref, v_ref, copies_ref, kv_ref):
    kv_ref[:, :HD] = k_ref[...]
    kv_ref[:, HD:] = v_ref[...]
    for peer in range(PEERS):
        copies_ref[peer] = q_ref[...]


def prepare(q, k, v):
    vmem = pl.BlockSpec(memory_space=pltpu.VMEM)
    return pl.pallas_call(
        prepare_kernel,
        out_shape=(
            jax.ShapeDtypeStruct((PEERS,) + q.shape, q.dtype),
            jax.ShapeDtypeStruct((k.shape[0], 2 * HD), k.dtype),
        ),
        in_specs=[vmem] * 3,
        out_specs=(vmem, vmem),
        name="prepare",
    )(q, k, v)


def attend_kernel(
    meta, caps, lengths, q_ref, kv_ref, new_k_ref, new_v_ref, out_ref, acc_ref, totals_ref
):
    totals_ref[...] = jnp.zeros_like(totals_ref)

    def serve(peer):
        tokens = q_ref.shape[1]
        new_keys = new_k_ref.shape[0]
        z_base, my_z0, my_yh = meta[0], meta[1], meta[2]
        peer_z0 = peer // 2
        peer_yh = peer % 2
        request = z_base + peer_z0
        cap = jnp.full((1, 1), caps[request], jnp.float32)
        inner = SCALE / cap
        outer = cap * LOG2E
        slot = peer
        q = jnp.concatenate(
            [q_ref[slot, :, h * HD : (h + 1) * HD].astype(jnp.bfloat16) for h in range(GROUP)], axis=0
        )

        def weigh(k):
            raw = lax.dot_general(
                q, k, (((1,), (1,)), ((), ())), preferred_element_type=jnp.float32
            )
            return jnp.exp2(outer * jnp.tanh(raw * inner))

        def gather(w, v):
            return jnp.dot(
                w.astype(jnp.bfloat16),
                jnp.concatenate([v, jnp.ones_like(v)], axis=1),
                preferred_element_type=jnp.float32,
            )

        def document():
            return gather(weigh(kv_ref[:, :HD]), kv_ref[:, HD:])

        def suffix():
            w = weigh(new_k_ref[...])
            place = lax.broadcasted_iota(jnp.int32, w.shape, 0) % tokens
            row = peer_yh * tokens + place
            col = my_yh * new_keys + lax.broadcasted_iota(jnp.int32, w.shape, 1)
            seen = (col <= row) & (col < lengths[request])
            return gather(jnp.where(seen, w, 0.0), new_v_ref[...])

        sees_suffix = (peer_z0 == my_z0) & (peer_yh >= my_yh)

        @pl.when(sees_suffix)
        def _():
            acc_ref[...] = suffix() + document()

        @pl.when(jnp.logical_not(sees_suffix))
        def _():
            acc_ref[...] = document()

        groups = tokens // (2 * PIECE)
        for head in range(GROUP):
            cols = slice(head * HD, (head + 1) * HD)
            for c in range(2):
                rows = [head * tokens + (2 * j + c) * PIECE for j in range(groups)]
                for j in range(groups):
                    out_ref[2 * peer + c, j * PIECE : (j + 1) * PIECE, cols] = acc_ref[
                        rows[j] : rows[j] + PIECE, :HD
                    ].astype(out_ref.dtype)
                totals = jnp.concatenate([acc_ref[r : r + PIECE, HD:] for r in rows], axis=0)
                lane = lax.broadcasted_iota(jnp.int32, totals.shape, 1)
                place = (2 * peer + c) * GROUP + head
                totals_ref[...] = jnp.where(lane == place, totals, totals_ref[...])

    for peer in range(PEERS):
        serve(peer)

    low_rows = totals_ref[...].T[: 2 * PEERS * GROUP]
    high_rows = low_rows.astype(jnp.bfloat16).astype(jnp.float32)
    low_rows = low_rows - high_rows
    first = lax.broadcasted_iota(jnp.int32, (META, HD), 0) == 0
    for target in range(2 * PEERS):
        for head in range(GROUP):
            row = slice(target * GROUP + head, target * GROUP + head + 1)
            pair = jnp.where(first, high_rows[row], low_rows[row])
            out_ref[target, out_ref.shape[1] - META :, head * HD : (head + 1) * HD] = pair.astype(
                out_ref.dtype
            )


def attend(meta, caps, lengths, q, kv, new_k, new_v):
    _, tokens, _ = q.shape
    keys = kv.shape[0]
    smem = pl.BlockSpec(memory_space=pltpu.SMEM)
    vmem = pl.BlockSpec(memory_space=pltpu.VMEM)
    elements = PEERS * tokens * GROUP * (keys + new_k.shape[0] // 2)
    return pl.pallas_call(
        attend_kernel,
        out_shape=jax.ShapeDtypeStruct(
            (PEERS * 2, tokens // 2 + META, GROUP * HD), jnp.bfloat16
        ),
        in_specs=[smem, smem, smem, vmem, vmem, vmem, vmem],
        out_specs=vmem,
        scratch_shapes=[
            pltpu.VMEM((GROUP * tokens, 2 * HD), jnp.float32),
            pltpu.VMEM((tokens // 2, HD), jnp.float32),
        ],
        compiler_params=pltpu.CompilerParams(
            vmem_limit_bytes=40 * 1024 * 1024,
        ),
        cost_estimate=pl.CostEstimate(
            flops=elements * HD * 4,
            bytes_accessed=4 * 1024 * 1024,
            transcendentals=elements * 2,
        ),
        name="attend",
    )(meta, caps, lengths, q, kv, new_k, new_v)


def project_kernel(meta, parts_ref, mine_ref, other_ref, out_ref):
    half = parts_ref.shape[1] - META
    sources = parts_ref.shape[0] // 2
    own_core = meta[3]

    def mix(core):
        heads = []
        for head in range(GROUP):
            cols = slice(head * HD, (head + 1) * HD)
            summed = jnp.zeros((half, HD), jnp.float32)
            totals = jnp.zeros((1, HD), jnp.float32)
            for s in range(sources):
                summed += parts_ref[2 * s + core, :half, cols].astype(jnp.float32)
                pair = parts_ref[2 * s + core, half:, cols].astype(jnp.float32)
                totals += pair[0:1] + pair[1:2]
            column = jnp.broadcast_to(totals, (HD, HD)).T
            heads.append((summed / column).astype(jnp.bfloat16))
        return jnp.concatenate(heads, axis=1)

    mine = mix(own_core)
    other = mix(1 - own_core)
    width = out_ref.shape[1]
    for start in range(0, width, BLOCK):
        cols = slice(start, start + BLOCK)
        total = jnp.dot(mine, mine_ref[:, cols], preferred_element_type=jnp.float32)
        total += jnp.dot(other, other_ref[:, cols], preferred_element_type=jnp.float32)
        out_ref[:, cols] = total.astype(out_ref.dtype)


def project(meta, parts, mine, other):
    half = parts.shape[1] - META
    depth, width = mine.shape
    vmem = pl.BlockSpec(memory_space=pltpu.VMEM)
    return pl.pallas_call(
        project_kernel,
        out_shape=jax.ShapeDtypeStruct((half, width), jnp.bfloat16),
        in_specs=[pl.BlockSpec(memory_space=pltpu.SMEM), vmem, vmem, vmem],
        out_specs=vmem,
        compiler_params=pltpu.CompilerParams(vmem_limit_bytes=40 * 1024 * 1024),
        cost_estimate=pl.CostEstimate(
            flops=4 * half * depth * width,
            bytes_accessed=8 * 1024 * 1024,
            transcendentals=0,
        ),
        name="project",
    )(meta, parts, mine, other)


def local(
    queries, prefix_keys, prefix_values, suffix_keys, suffix_values, out_weight, lengths, caps
):
    tokens = queries.shape[0]
    meta = jnp.stack(
        [
            lax.axis_index("z321") * 2,
            lax.axis_index("z0"),
            lax.axis_index("yh"),
            lax.axis_index("c"),
        ]
    ).astype(jnp.int32)
    copies, pair = prepare(queries, prefix_keys, prefix_values)
    q = lax.all_to_all(copies, QUERY_AXES, 0, 0, tiled=True)
    with jax.named_scope("document_gather"):
        kv = lax.all_gather(
            pair, KEY_AXES, axis=0, tiled=True
        )
    parts = attend(meta, caps, lengths, q, kv, suffix_keys, suffix_values)
    late_weight, parts = lax.optimization_barrier((out_weight, parts))
    with jax.named_scope("partials_to_owner"):
        parts = lax.all_to_all(parts, ("z0", "yh", "c"), 0, 0, tiled=True)
    weights = (out_weight, lax.ppermute(late_weight, "c", [(0, 1), (1, 0)]))
    partial = project(meta, parts, *weights)
    with jax.named_scope("heads_exchange"):
        pieces = lax.all_to_all(
            partial.reshape(8, PIECE, -1), ("yl", "x"), 0, 0, tiled=True
        )
    return jnp.sum(pieces.astype(jnp.float32), axis=0)


def solution(mesh):
    fine = Mesh(mesh.devices.reshape(SIZES), AXES)
    return jax.shard_map(
        local,
        mesh=fine,
        in_specs=(
            P(CTX, HEADS),
            P(CTX, HEADS),
            P(CTX, HEADS),
            P(CTX, HEADS),
            P(CTX, HEADS),
            P(HEADS, None),
            P(),
            P(),
        ),
        out_specs=P(CTX + HEADS, None),
        check_vma=False,
    )
```
